256 devices in a mesh: dp: 4 (over x), mp: 64 (over y, z, core).
Axes of the slice: x: 4, y: 4, z: 8, core: 2. Of those that a mesh axis runs over, the one named last changes fastest.
Arguments:
- tokens: bfloat16 [1024, 8192], P('dp', 'mp'), may hold values from -6 to 6
- gate_act: bfloat16 [1024, 16384], P('dp', 'mp'), may hold values from -6 to 6
- up_act: bfloat16 [1024, 16384], P('dp', 'mp'), may hold values from -6 to 6
- hidden_grad: bfloat16 [1024, 16384], P('dp', 'mp'), may hold values from -0.59765625 to 0.59765625
- gate_weight: bfloat16 [8192, 16384], P(None, 'mp'), may hold values from -0.375 to 0.375
- up_weight: bfloat16 [8192, 16384], P(None, 'mp'), may hold values from -0.375 to 0.375
- block_mask: int32 [2, 64, 128], replicated, may hold values from 0 to 1, as said below
- row_perm: int32 [2, 64], replicated, may hold values from 0 to 63, as said below
- scale_exp: int32 [2, 64, 128], replicated, may hold values from 1 to 2
Outputs:
- input_grad: bfloat16 [1024, 8192], P('dp', 'mp')
- weight_grads: float32 [2, 8192, 16384], P(None, ('mp', 'dp'))
The draws below stay inside these ranges and needn't reach their ends.
Inputs may be any that keep to these rules, and one draw needn't show every extreme that they name: `block_mask`: within a row block, each of the 64 column groups of 2 block columns holds the same number of kept blocks, at most 1; positions k of row_perm from o * 1 to (o + 1) - 1 belong to owner o, and for each matrix all row blocks of some owner hold exactly 1 kept blocks in every column group. `row_perm`: for each matrix a permutation of the row blocks.
All inputs are finite; a program needn't handle non-finite values.
Results may differ from the reference program's by a relative error of at most 0.012.
Values may be sent and summed in bfloat16 or wider, within the bound.
A program may use at most 128 MiB of HBM per device.

```python
import jax
import jax.numpy as jnp
from jax import lax

D = 8192
FF = 16384
BLOCK = 128
TOK_DEV = 256
TOKENS = 1024
RBLOCKS = 64
CBLOCKS = 128
ROW_OWN = 1
COL_OWN = 2
N_DP = 4
N_MP = 64


def shared_pattern(key):
    perms = jnp.stack([jax.random.permutation(jax.random.fold_in(key, 11 + which), RBLOCKS) for which in range(2)]).astype(jnp.int32)
    hottest = jax.random.randint(jax.random.fold_in(key, 21), (2,), 0, N_MP)
    inverse = jnp.argsort(perms, axis=1).astype(jnp.int32)
    owners = inverse // ROW_OWN
    levels = jax.random.randint(jax.random.fold_in(key, 31), (2, RBLOCKS), 0, COL_OWN // 2 + 1)
    levels = jnp.where(owners == hottest[:, None], COL_OWN // 2, levels)
    scores = jax.random.randint(jax.random.fold_in(key, 41), (2, RBLOCKS, N_MP, COL_OWN), 0, 1 << 20) * COL_OWN
    scores = scores + jnp.arange(COL_OWN, dtype=jnp.int32)
    ranks = jnp.argsort(jnp.argsort(scores, axis=-1), axis=-1)
    live = (ranks < levels[:, :, None, None]).astype(jnp.int32).reshape(2, RBLOCKS, CBLOCKS)
    return (live, perms)


def draw_block_mask(key, part):
    live, perms = shared_pattern(key)
    return live


def draw_row_perm(key, part):
    live, perms = shared_pattern(key)
    return perms


def set_ends(entries, stream_key, low, largest):
    spot = [jax.random.randint(jax.random.fold_in(stream_key, axis), (), 0, length) for axis, length in enumerate(entries.shape)]
    longest = entries.shape.index(max(entries.shape))
    next_to = spot[:longest] + [(spot[longest] + 1) % entries.shape[longest]] + spot[longest + 1:]
    return entries.at[tuple(spot)].set(low).at[tuple(next_to)].set(largest)


def steps_of(rng, extent, split, smallest, top_value):
    def one(axis_at, shards_of):
        heights = jax.random.uniform(jax.random.fold_in(jax.random.fold_in(rng, 6), axis_at), (shards_of,), jnp.float32, smallest / len(split), top_value / len(split))
        return jnp.repeat(jnp.exp(heights), extent[axis_at] // shards_of).reshape((-1,) + (1,) * (len(extent) - axis_at - 1))

    gain = one(*split[0])
    for cut in split[1:]:
        gain = gain * one(*cut)
    return gain


def gaussian(key, shape, width, bound, cuts=(), held_as=jnp.bfloat16):
    drawn = width * jax.random.normal(key, shape, jnp.float32)
    if cuts:
        drawn = drawn * steps_of(key, shape, cuts, -0.22, 0.18)
    return jnp.clip(drawn, -bound, bound).astype(held_as)


def setup_inputs(seed: int = 0) -> dict:
    arg_keys = jax.random.split(jax.random.key(seed), 10)
    tokens = gaussian(arg_keys[0], (TOKENS, D), 1.0, 6.0, ((0, 4), (1, 64)))
    gate_act = gaussian(arg_keys[1], (TOKENS, FF), 1.0, 6.0, ((0, 4), (1, 64)))
    up_act = gaussian(arg_keys[2], (TOKENS, FF), 1.0, 6.0, ((0, 4), (1, 64)))
    hidden_grad = gaussian(arg_keys[3], (TOKENS, FF), 0.1, 0.59765625, ((0, 4), (1, 64)))
    gate_weight = gaussian(arg_keys[4], (D, FF), (FF // 64) ** -0.5, 0.375, ((1, 64),))
    up_weight = gaussian(arg_keys[5], (D, FF), (FF // 64) ** -0.5, 0.375, ((1, 64),))
    block_mask = draw_block_mask(jax.random.fold_in(arg_keys[9], 71), 0)
    row_perm = draw_row_perm(jax.random.fold_in(arg_keys[9], 71), 0)
    scale_exp = set_ends(jax.random.randint(arg_keys[8], (2, RBLOCKS, CBLOCKS), min(1, TOK_DEV // 32) + min(1, TOK_DEV // 128) + min(1, TOK_DEV // 512) + min(1, TOK_DEV // 2048) - 1, min(1, TOK_DEV // 32) + min(1, TOK_DEV // 128) + min(1, TOK_DEV // 512) + min(1, TOK_DEV // 2048) + 1), jax.random.fold_in(arg_keys[8], 1), min(1, TOK_DEV // 32) + min(1, TOK_DEV // 128) + min(1, TOK_DEV // 512) + min(1, TOK_DEV // 2048) - 1, (min(1, TOK_DEV // 32) + min(1, TOK_DEV // 128) + min(1, TOK_DEV // 512) + min(1, TOK_DEV // 2048) + 1) - 1).astype(jnp.int32)
    return dict(tokens=tokens, gate_act=gate_act, up_act=up_act, hidden_grad=hidden_grad, gate_weight=gate_weight, up_weight=up_weight, block_mask=block_mask, row_perm=row_perm, scale_exp=scale_exp)


def expand(blocks):
    return jnp.repeat(jnp.repeat(blocks, BLOCK, 0), BLOCK, 1)


def reference(tokens, gate_act, up_act, hidden_grad, gate_weight, up_weight, block_mask, row_perm, scale_exp):
    gate_f = gate_act.astype(jnp.float32)
    up_f = up_act.astype(jnp.float32)
    hid_f = hidden_grad.astype(jnp.float32)
    sig = jax.nn.sigmoid(gate_f)
    gate_grad = (hid_f * up_f * sig * (1.0 + gate_f * (1.0 - sig))).astype(jnp.bfloat16)
    up_grad = (hid_f * gate_f * sig).astype(jnp.bfloat16)
    dims = (((1,), (1,)), ((), ()))
    weights = [gate_weight, up_weight]
    grads_in = [gate_grad, up_grad]
    input_grad = jnp.zeros((TOKENS, D), jnp.float32)
    results = []
    for which in range(2):
        mask = expand(block_mask[which]).astype(jnp.bfloat16)
        masked = weights[which] * mask
        input_grad = input_grad + lax.dot_general(grads_in[which], masked, dims, preferred_element_type=jnp.float32)
        down_scale = jnp.exp2(-expand(scale_exp[which]).astype(jnp.float32))
        total = jnp.zeros((D, FF), jnp.float32)
        for group in range(N_DP):
            rows = tokens[group * TOK_DEV:(group + 1) * TOK_DEV]
            local = grads_in[which][group * TOK_DEV:(group + 1) * TOK_DEV]
            partial_grad = lax.dot_general(rows, local, (((0,), (0,)), ((), ())), preferred_element_type=jnp.float32)
            partial_grad = partial_grad * mask.astype(jnp.float32)
            clipped = jnp.clip(partial_grad * down_scale, -1.0, 1.0).astype(jnp.bfloat16)
            clipped = lax.optimization_barrier(clipped)
            total = total + clipped.astype(jnp.float32)
        grads = total / down_scale
        order = (row_perm[which][:, None] * BLOCK + jnp.arange(BLOCK, dtype=jnp.int32)[None, :]).reshape(D)
        results.append(jnp.take(grads, order.astype(jnp.int32), axis=0))
    return input_grad.astype(jnp.bfloat16), jnp.stack(results)
```

```python
import functools

import jax
import jax.numpy as jnp
from jax import lax
from jax.experimental import pallas as pl
from jax.experimental.pallas import tpu as pltpu
from jax.sharding import PartitionSpec as P

BF = jnp.bfloat16
F32 = jnp.float32
MESH = pl.DeviceIdType.MESH
NX, NY, NZ, NC = 4, 4, 8, 2
NM = NY * NZ * NC
HALF = 16
N_SEM = 96


def slot_of(o):
    return jnp.where(o <= 3, 2 * o, jnp.where(o == 4, 7, 2 * (8 - o) - 1))


def static_slot(o):
    o %= 8
    return 2 * o if o <= 3 else (7 if o == 4 else 2 * (8 - o) - 1)


def kernel(
    tok_ref, g_ref, u_ref, h_ref, wg_ref, wu_ref, mask_ref, perm_ref, exp_ref,
    ig_ref, recv_ref, fac_ref,
    tok, gact, uact, hgrad, wg, wu, xsrc, tt0, tt1, G, GT, wm, facx, lhs, fs, abuf,
    part, crecv, ysum, yrA, yrB, yr2m, yr2p, zr,
    ss, rs, a_ss, a_rs, lsem,
):
    q = lax.axis_index("dp")
    m = lax.axis_index("mp")
    c = lax.rem(m, NC)
    z = lax.rem(lax.div(m, NC), NZ)
    y = lax.div(m, NC * NZ)
    yp, ym, yo = lax.rem(y + 1, NY), lax.rem(y + 3, NY), lax.rem(y + 2, NY)

    def mp_of(yy, zz, cc):
        return (yy * NZ + zz) * NC + cc

    dev_yp, dev_ym = (q, mp_of(yp, z, c)), (q, mp_of(ym, z, c))
    dev_sib = (q, mp_of(y, z, 1 - c))

    def dev_z(d):
        return (q, mp_of(y, lax.rem(z + d, NZ), c))

    def dev_x(d):
        return (lax.rem(q + d, NX), m)

    tts = (tt0, tt1)

    loads = []
    for i, (src, dst) in enumerate(
        ((tok_ref, tok), (g_ref, gact), (u_ref, uact), (h_ref, hgrad))
    ):
        cp = pltpu.make_async_copy(src, dst, lsem.at[i])
        cp.start()
        loads.append(cp)
    wloads = []
    for i, (src, dst) in enumerate(((wg_ref, wg), (wu_ref, wu))):
        cp = pltpu.make_async_copy(src, dst, lsem.at[4 + i])
        cp.start()
        wloads.append(cp)

    barrier = pltpu.get_barrier_semaphore()

    def greet(i, carry):
        pl.semaphore_signal(
            barrier, inc=1, device_id=(q, lax.rem(m + i, NM)), device_id_type=MESH
        )
        return carry

    lax.fori_loop(1, NM, greet, 0)
    for d in range(1, NX):
        pl.semaphore_signal(barrier, inc=1, device_id=dev_x(d), device_id_type=MESH)

    loads[0].wait()
    tok_t = tok[...].T
    for h in range(2):
        for k in range(NX):
            xsrc[h, k] = tok_t[32 * k + HALF * h : 32 * k + HALF * (h + 1), :]
        tts[h][c, y, 0, q] = xsrc[h, q]

    pl.semaphore_wait(barrier, NM - 1 + NX - 1)

    sent = []

    def send(src, dst, dev):
        i = len(sent)
        cp = pltpu.make_async_remote_copy(
            src_ref=src, dst_ref=dst, send_sem=ss.at[i], recv_sem=rs.at[i],
            device_id=dev, device_id_type=MESH,
        )
        cp.start()
        sent.append(cp)
        return cp

    xcp = [[], []]
    for h in range(2):
        for d in (1, 3, 2):
            to = lax.rem(q + d, NX)
            xcp[h].append(send(xsrc.at[h, to], tts[h].at[c, y, 0, q], dev_x(d)))

    for cp in loads[1:]:
        cp.wait()
    gf = gact[...].astype(F32)
    hf = hgrad[...].astype(F32)
    sig = jax.nn.sigmoid(gf)
    gg = (hf * uact[...].astype(F32) * sig * (1.0 + gf * (1.0 - sig))).astype(BF)
    ug = (hf * gf * sig).astype(BF)
    G[q, 0] = gg
    G[q, 1] = ug

    zcp = [{}, {}]

    def ag_start(h):
        for cp in xcp[h]:
            cp.wait_recv()
        t = tts[h]
        for d in (1, 7, 2, 6, 3, 5, 4):
            zcp[h][d] = send(
                t.at[c, y, 0], t.at[c, y, static_slot(-d)], dev_z(d)
            )

    groups = ((0, 1, ()), (1, 3, (1, 7)), (3, 8, (2, 6, 3, 5, 4)))
    ycp = [{}, {}]
    ocp = [{}, {}]
    scp = [[], []]

    def ag_y(h, gi):
        s0, s1, ds = groups[gi]
        for d in ds:
            zcp[h][d].wait_recv()
        t = tts[h]
        src = t.at[c, y, pl.ds(s0, s1 - s0)]
        ycp[h][gi] = (send(src, src, dev_yp), send(src, src, dev_ym))

    def ag_o(h, gi):
        s0, s1, _ = groups[gi]
        t = tts[h]
        ycp[h][gi][0].wait_recv()
        a = t.at[c, ym, pl.ds(s0, s1 - s0), pl.ds(0, 2)]
        first = send(a, a, dev_yp)
        ycp[h][gi][1].wait_recv()
        b = t.at[c, yp, pl.ds(s0, s1 - s0), pl.ds(2, 2)]
        ocp[h][gi] = (first, send(b, b, dev_ym))

    def ag_sib(h, col):
        r = tts[h].at[c, col]
        scp[h].append(send(r, r, dev_sib))

    ag_start(0)
    ag_y(0, 0)
    for d in (1, 3, 2):
        to = q
        send(G.at[q], G.at[to], dev_x(d))
    gcp = sent[-3:]
    ag_start(1)

    lane = lax.broadcasted_iota(jnp.int32, (2, NM, 128), 2)
    for j in range(2):
        pick = lane == 2 * m + j
        mk = jnp.sum(jnp.where(pick, mask_ref[...], 0).astype(F32), axis=2, keepdims=True)
        ex = jnp.sum(jnp.where(pick, exp_ref[...], 0).astype(F32), axis=2, keepdims=True)
        mkb = jnp.broadcast_to(mk, (2, NM, 128))
        facx[:, j] = mkb * jnp.exp2(-jnp.broadcast_to(ex, (2, NM, 128)))
        wm[:, :, 128 * j : 128 * (j + 1)] = mkb
    for w in range(2):
        row = perm_ref[w, m]
        mrow = mask_ref[w, pl.ds(row, 1), :].astype(F32)
        erow = exp_ref[w, pl.ds(row, 1), :].astype(F32)
        fac_ref[w : w + 1, :] = mrow * jnp.exp2(erow)

    GT[0:256] = gg.T
    GT[256:512] = ug.T
    for cp in wloads:
        cp.wait()

    def ig_chunk(yy):
        def step(i, carry):
            blk = yy * 16 + i * 8
            rows = pl.ds(pl.multiple_of(blk * 128, 1024), 1024)
            acc = None
            for w, wref in enumerate((wg, wu)):
                mrows = wm[w, pl.ds(pl.multiple_of(blk, 8), 8), :].astype(BF)
                wv = wref[rows, :].reshape(8, 128, 256) * mrows[:, None, :]
                r = jnp.dot(
                    wv.reshape(1024, 256), GT[256 * w : 256 * (w + 1)],
                    preferred_element_type=F32,
                )
                acc = r if acc is None else acc + r
            acc = acc.astype(BF).reshape(4, 2, 128, 256)
            for cc in range(2):
                part[cc, yy, pl.ds(i * 4, 4)] = acc[:, cc]
            return carry

        lax.fori_loop(0, 2, step, 0)
        return send(part.at[1 - c, yy], crecv.at[yy], dev_sib)

    ccp = {}
    ccp["o"] = ig_chunk(yo)
    ag_y(0, 1)
    ccp["p"] = ig_chunk(yp)
    ag_y(0, 2)
    ag_sib(0, y)
    ag_y(1, 0)
    ag_o(0, 0)
    ccp["m"] = ig_chunk(ym)
    ag_y(1, 1)
    ag_o(0, 1)
    ccp["s"] = ig_chunk(y)

    def csum(yy):
        for zz in range(NZ):
            v = part[c, yy, zz].astype(F32) + crecv[yy, zz].astype(F32)
            ysum[yy, zz] = v.astype(BF)

    ag_y(1, 2)
    ag_sib(1, y)
    ag_o(0, 2)
    ag_sib(0, ym)
    ag_sib(0, yp)

    ccp["o"].wait_recv()
    csum(yo)
    rcpA = send(ysum.at[yo, pl.ds(0, 4)], yrA, dev_yp)
    rcpB = send(ysum.at[yo, pl.ds(4, 4)], yrB, dev_ym)

    ag_o(1, 0)
    ag_o(1, 1)
    for gi in range(3):
        ocp[0][gi][0].wait_recv()
        ocp[0][gi][1].wait_recv()
    ag_sib(0, yo)
    ag_o(1, 2)
    ag_sib(1, ym)
    ag_sib(1, yp)
    for cp in gcp:
        cp.wait_recv()
    for cp in scp[0]:
        cp.wait_recv()

    def wgrad(h):
        t = tts[h]

        def group(gi, carry):
            for w in range(2):
                def gather(i, carry2):
                    k = lax.rem(m + gi * 16 + i, NM)
                    b = perm_ref[w, k]
                    cc = lax.rem(b, NC)
                    zz = lax.rem(lax.div(b, NC), NZ)
                    yy = lax.div(b, NC * NZ)
                    o = lax.rem(zz + NZ - z, NZ)
                    rows = pl.ds(pl.multiple_of(i * HALF, HALF), HALF)
                    lhs[w, :, rows, :] = t[cc, yy, slot_of(o)]
                    for j in range(2):
                        fs[w, j, rows, :] = jnp.broadcast_to(
                            facx[w, j, pl.ds(b, 1), :], (HALF, 128)
                        )
                    return carry2

                lax.fori_loop(0, 16, gather, 0, unroll=True)
                tot = None
                for p in range(NX):
                    r = jnp.dot(lhs[w, p], G[p, w], preferred_element_type=F32)
                    v = r[:, :128] * fs[w, 0] + r[:, 128:] * fs[w, 1]
                    v = jnp.clip(v, -1.0, 1.0).astype(BF).astype(F32)
                    tot = v if tot is None else tot + v
                abuf[h, pl.ds(gi * 16, 16), w] = tot.astype(BF).reshape(16, HALF, 128)

            def push(i, carry2):
                k = lax.rem(m + i, NM)

                @pl.when(i > 0)
                def _():
                    pltpu.make_async_remote_copy(
                        src_ref=abuf.at[h, i], dst_ref=recv_ref.at[h, m],
                        send_sem=a_ss.at[h], recv_sem=a_rs.at[h],
                        device_id=(q, k), device_id_type=MESH,
                    ).start()

                return carry2

            lax.fori_loop(gi * 16, gi * 16 + 16, push, 0)
            return carry

        lax.fori_loop(0, 4, group, 0)

    wgrad(0)
    own = []
    cp = pltpu.make_async_copy(abuf.at[0, 0], recv_ref.at[0, m], lsem.at[6])
    cp.start()
    own.append(cp)

    ccp["p"].wait_recv()
    ccp["m"].wait_recv()
    csum(yp)
    csum(ym)
    rcpA.wait_recv()
    for i in range(4):
        ysum[yp, i] = (ysum[yp, i].astype(F32) + yrA[i].astype(F32)).astype(BF)
    r2p = send(ysum.at[yp], yr2m, dev_yp)
    rcpB.wait_recv()
    for i in range(4):
        ysum[ym, 4 + i] = (ysum[ym, 4 + i].astype(F32) + yrB[i].astype(F32)).astype(BF)
    r2m = send(ysum.at[ym], yr2p, dev_ym)

    for gi in range(3):
        ocp[1][gi][0].wait_recv()
        ocp[1][gi][1].wait_recv()
    ag_sib(1, yo)
    for cp in scp[1]:
        cp.wait_recv()
    wgrad(1)
    cp = pltpu.make_async_copy(abuf.at[1, 0], recv_ref.at[1, m], lsem.at[7])
    cp.start()
    own.append(cp)

    ccp["s"].wait_recv()
    r2p.wait_recv()
    r2m.wait_recv()
    for i in range(NZ):
        v = part[c, y, i].astype(F32) + crecv[y, i].astype(F32)
        v = v + yr2m[i].astype(F32) + yr2p[i].astype(F32)
        ysum[y, i] = v.astype(BF)
    zc = []
    for d in range(1, NZ):
        zc.append(send(ysum.at[y, lax.rem(z + d, NZ)], zr.at[d - 1], dev_z(d)))
    tot = ysum[y, z].astype(F32)
    for d in range(1, NZ):
        zc[d - 1].wait_recv()
        tot = tot + zr[d - 1].astype(F32)
    ig_ref[...] = tot.T.astype(BF)

    for cp in own:
        cp.wait()
    for h in range(2):
        done = pltpu.make_async_remote_copy(
            src_ref=abuf.at[h, pl.ds(1, NM - 1)], dst_ref=recv_ref.at[h, pl.ds(0, NM - 1)],
            send_sem=a_ss.at[h], recv_sem=a_rs.at[h], device_id=dev_sib, device_id_type=MESH,
        )
        done.wait_recv()
        done.wait_send()
    for cp in sent:
        cp.wait_send()


def expand(recv_ref, fac_ref, out_ref):
    g = pl.program_id(0)
    for s in range(8):
        for w in range(2):
            for h in range(2):
                v = recv_ref[h, s, w].astype(F32)
                for j in range(2):
                    col = (s * 2 + j) * 128
                    f = fac_ref[w, (g * 8 + s) * 2 + j]
                    out_ref[w, h * HALF : (h + 1) * HALF, col : col + 128] = v * f


def body(tokens, gate_act, up_act, hidden_grad, gate_weight, up_weight, block_mask, row_perm, scale_exp):
    any_spec = pl.BlockSpec(memory_space=pl.ANY)
    vm = pl.BlockSpec(memory_space=pltpu.VMEM)
    sm = pl.BlockSpec(memory_space=pltpu.SMEM)
    V = pltpu.VMEM
    tt = V((2, NY, NZ, NX, HALF, 256), BF)
    ig, recv, fac = pl.pallas_call(
        kernel,
        out_shape=(
            jax.ShapeDtypeStruct((256, 128), BF),
            jax.ShapeDtypeStruct((2, NM, 2, HALF, 128), BF),
            jax.ShapeDtypeStruct((2, 128), F32),
        ),
        in_specs=[any_spec] * 6 + [vm, sm, vm],
        out_specs=(vm, any_spec, vm),
        scratch_shapes=[
            V((256, 128), BF), V((256, 256), BF), V((256, 256), BF), V((256, 256), BF),
            V((8192, 256), BF), V((8192, 256), BF),
            V((2, NX, HALF, 256), BF), tt, tt,
            V((NX, 2, 256, 256), BF), V((512, 256), BF),
            V((2, NM, 256), F32), V((2, 2, NM, 128), F32),
            V((2, NX, 256, 256), BF), V((2, 2, 256, 128), F32),
            V((2, NM, 2, HALF, 128), BF),
            V((2, NY, NZ, 128, 256), BF), V((NY, NZ, 128, 256), BF), V((NY, NZ, 128, 256), BF),
            V((4, 128, 256), BF), V((4, 128, 256), BF), V((NZ, 128, 256), BF), V((NZ, 128, 256), BF),
            V((NZ - 1, 128, 256), BF),
            pltpu.SemaphoreType.DMA((N_SEM,)), pltpu.SemaphoreType.DMA((N_SEM,)),
            pltpu.SemaphoreType.DMA((2,)), pltpu.SemaphoreType.DMA((2,)),
            pltpu.SemaphoreType.DMA((8,)),
        ],
        compiler_params=pltpu.CompilerParams(
            collective_id=0, has_side_effects=True, vmem_limit_bytes=56 << 20
        ),
        name="grads",
    )(tokens, gate_act, up_act, hidden_grad, gate_weight, up_weight, block_mask, row_perm, scale_exp)
    out = pl.pallas_call(
        expand,
        grid=(8,),
        out_shape=jax.ShapeDtypeStruct((2, 32, 16384), F32),
        in_specs=[pl.BlockSpec((2, 8, 2, HALF, 128), lambda i: (0, i, 0, 0, 0)), sm],
        out_specs=pl.BlockSpec((2, 32, 2048), lambda i: (0, 0, i)),
        name="expand",
    )(recv, fac)
    return ig, out


def solution(mesh):
    act = P("dp", "mp")
    weight = P(None, "mp")
    in_specs = (act, act, act, act, weight, weight, P(), P(), P())
    out_specs = (act, P(None, ("mp", "dp"), None))
    return jax.shard_map(body, mesh=mesh, in_specs=in_specs, out_specs=out_specs, check_vma=False)
```

```python
import jax
import jax.numpy as jnp
from jax import lax
from jax.experimental import pallas as pl
from jax.experimental.pallas import tpu as pltpu
from jax.sharding import PartitionSpec as P

BF = jnp.bfloat16
F32 = jnp.float32
MESH = pl.DeviceIdType.MESH
NX, NY, NZ, NC = 4, 4, 8, 2
NM = NY * NZ * NC
HALF = 16
N_SEM = 96


def slot_of(o):
    return jnp.where(o <= 3, 2 * o, jnp.where(o == 4, 7, 2 * (8 - o) - 1))


def static_slot(o):
    o %= 8
    return 2 * o if o <= 3 else (7 if o == 4 else 2 * (8 - o) - 1)


SCHEDULE = (
    ("xt",), ("ga",), ("zs",), ("y", 0), ("ys",), ("gx",), ("mk",), ("il",), ("i", "o"), ("i", "p"),
    ("y", 1), ("i", "m"), ("i", "s"), ("k", 1), ("bk", 0), ("c", "o"), ("r1",), ("o", 0), ("y", 2),
    ("b", "s"), ("k", 2), ("bk", 1), ("o", 1), ("c", "p"), ("c", "m"), ("c", "s"), ("o", 2),
    ("k", 3), ("bk", 2), ("r2",), ("b", "m"), ("b", "p"), ("k", 4), ("bk", 3), ("b", "o"), ("w", 0),
    ("bk", 4), ("w", 1, 0, 1), ("rz", 4), ("w", 1, 1, 2), ("rz", 3), ("w", 1, 2, 3), ("rz", 2),
    ("w", 1, 3, 4), ("rz", 1), ("rz", 0),
)


def kernel(
    tok_ref, g_ref, u_ref, h_ref, wg_ref, wu_ref, mask_ref, perm_ref, exp_ref,
    ig_ref, recv_ref, fac_ref,
    tok, gact, uact, hgrad, wg, wu, xsrc, tt0, tt1, G, GT, wm, facx, lhs, fs, abuf,
    part, crecv, ysum, yrA, yrB, yr2m, yr2p, zra, zrb, zr,
    ss, rs, a_ss, a_rs, lsem,
):
    q = lax.axis_index("dp")
    m = lax.axis_index("mp")
    c = lax.rem(m, NC)
    z = lax.rem(lax.div(m, NC), NZ)
    y = lax.div(m, NC * NZ)
    yp, ym, yo = lax.rem(y + 1, NY), lax.rem(y + 3, NY), lax.rem(y + 2, NY)

    def mp_of(yy, zz, cc):
        return (yy * NZ + zz) * NC + cc

    dev_yp, dev_ym = (q, mp_of(yp, z, c)), (q, mp_of(ym, z, c))
    dev_sib = (q, mp_of(y, z, 1 - c))

    def dev_z(d):
        return (q, mp_of(y, lax.rem(z + d, NZ), c))

    def dev_x(d):
        return (lax.rem(q + d, NX), m)

    loads = []
    for i, (src, dst) in enumerate(
        ((tok_ref, tok), (g_ref, gact), (u_ref, uact), (h_ref, hgrad))
    ):
        cp = pltpu.make_async_copy(src, dst, lsem.at[i])
        cp.start()
        loads.append(cp)
    wloads = []
    for i, (src, dst) in enumerate(((wg_ref, wg), (wu_ref, wu))):
        cp = pltpu.make_async_copy(src, dst, lsem.at[4 + i])
        cp.start()
        wloads.append(cp)

    barrier = pltpu.get_barrier_semaphore()

    partners = [dev_sib] + [dev_z(d) for d in range(1, NZ)] + [dev_x(d) for d in range(1, NX)]
    partners += [(q, mp_of(lax.rem(y + d, NY), z, c)) for d in range(1, NY)]
    for dev in partners:
        pl.semaphore_signal(barrier, inc=1, device_id=dev, device_id_type=MESH)

    sent = []

    class Remote:
        def __init__(self, src, dst, dev):
            i = len(sent)
            self.copy = pltpu.make_async_remote_copy(
                src_ref=src, dst_ref=dst, send_sem=ss.at[i], recv_sem=rs.at[i],
                device_id=dev, device_id_type=MESH,
            )
            self.copy.start()
            self.pending = True
            sent.append(self)

        def recv(self):
            if self.pending:
                self.copy.wait_recv()
                self.pending = False

    X, Z, Y, O, K, S, I, R = ({} for _ in range(8))
    own = []
    cols = {"s": y, "p": yp, "m": ym, "o": yo}

    def own_block(h):
        return tt0.at[c, y, 0] if h == 0 else tt1.at[c, 0, y]

    def x_tokens():
        loads[0].wait()
        tok_t = tok[...].T
        for h in range(2):
            for k in range(NX):
                xsrc[h, k] = tok_t[32 * k + HALF * h : 32 * k + HALF * (h + 1), :]
            own_block(h)[q] = xsrc[h, q]
        pl.semaphore_wait(barrier, len(partners))
        for h in range(2):
            for d in (1, 3, 2):
                to = lax.rem(q + d, NX)
                X[h, d] = Remote(xsrc.at[h, to], own_block(h).at[q], dev_x(d))

    def z_start():
        for d in (1, 3, 2):
            X[0, d].recv()
        for d in (1, 7, 2, 6, 3, 5, 4):
            Z[d] = Remote(tt0.at[c, y, 0], tt0.at[c, y, static_slot(-d)], dev_z(d))

    groups = ((0, 1, ()), (1, 3, (1, 7)), (3, 8, (2, 6, 3, 5, 4)))

    def y_first(g):
        s0, s1, ds = groups[g]
        for d in ds:
            Z[d].recv()
        r = tt0.at[c, y, pl.ds(s0, s1 - s0)]
        Y[g, "m"] = Remote(r, r, dev_yp)
        Y[g, "p"] = Remote(r, r, dev_ym)

    def y_second(g):
        s0, s1, _ = groups[g]
        Y[g, "m"].recv()
        r = tt0.at[c, ym, pl.ds(s0, s1 - s0), pl.ds(0, 2)]
        O[g, 0] = Remote(r, r, dev_yp)
        Y[g, "p"].recv()
        r = tt0.at[c, yp, pl.ds(s0, s1 - s0), pl.ds(2, 2)]
        O[g, 1] = Remote(r, r, dev_ym)

    def sibling(col):
        for g in range(3):
            if col == "o":
                O[g, 0].recv()
                O[g, 1].recv()
            elif col != "s":
                Y[g, col].recv()
        r = tt0.at[c, cols[col]]
        S[0, col] = Remote(r, r, dev_sib)

    def y_start():
        for d in (1, 3, 2):
            X[1, d].recv()
        r = own_block(1)
        for d in (1, 3, 2):
            Y["k", d] = Remote(r, r, (q, mp_of(lax.rem(y + d, NY), z, c)))

    def k_recv(step):
        for way in (1, -1):
            for n in range(2):
                if (step, way, n) in K:
                    K[step, way, n].recv()

    def k_step(step):
        if step == 1:
            for d in (1, 3, 2):
                Y["k", d].recv()
        for n in range(2):
            for way in (1, -1):
                if step == 4 and (way == 1) != (n == 0):
                    continue
                if step > 1:
                    K[step - 1, way, n].recv()
                half = pl.ds(2 * n, 2)
                src = tt1.at[c, static_slot(-way * (step - 1)), half]
                dst = tt1.at[c, static_slot(-way * step), half]
                K[step, way, n] = Remote(src, dst, dev_z(way % NZ))

    def k_sibling(g):
        k_recv(g)
        s0, s1 = ((0, 1), (1, 3), (3, 5), (5, 7), (7, 8))[g]
        r = tt1.at[c, pl.ds(s0, s1 - s0)]
        S[1, g] = Remote(r, r, dev_sib)

    def act_grads():
        for cp in loads[1:]:
            cp.wait()
        gf = gact[...].astype(F32)
        hf = hgrad[...].astype(F32)
        sig = jax.nn.sigmoid(gf)
        gg = (hf * uact[...].astype(F32) * sig * (1.0 + gf * (1.0 - sig))).astype(BF)
        ug = (hf * gf * sig).astype(BF)
        G[q, 0] = gg
        G[q, 1] = ug
        GT[0:256] = gg.T
        GT[256:512] = ug.T

    def x_grads():
        for d in (1, 3, 2):
            X["g", d] = Remote(G.at[q], G.at[q], dev_x(d))

    def masks():
        lane = lax.broadcasted_iota(jnp.int32, (2, NM, 128), 2)
        for j in range(2):
            pick = lane == 2 * m + j
            mk = jnp.sum(jnp.where(pick, mask_ref[...], 0).astype(F32), axis=2, keepdims=True)
            ex = jnp.sum(jnp.where(pick, exp_ref[...], 0).astype(F32), axis=2, keepdims=True)
            mkb = jnp.broadcast_to(mk, (2, NM, 128))
            facx[:, j] = mkb * jnp.exp2(-jnp.broadcast_to(ex, (2, NM, 128)))
            wm[:, :, 128 * j : 128 * (j + 1)] = mkb
        for w in range(2):
            row = perm_ref[w, m]
            mrow = mask_ref[w, pl.ds(row, 1), :].astype(F32)
            erow = exp_ref[w, pl.ds(row, 1), :].astype(F32)
            fac_ref[w : w + 1, :] = mrow * jnp.exp2(erow)

    def ig_load():
        for cp in wloads:
            cp.wait()

    def ig_chunk(col):
        yy = cols[col]

        def step(i, carry):
            blk = yy * 16 + i * 8
            rows = pl.ds(pl.multiple_of(blk * 128, 1024), 1024)
            acc = None
            for w, wref in enumerate((wg, wu)):
                mrows = wm[w, pl.ds(pl.multiple_of(blk, 8), 8), :].astype(BF)
                wv = wref[rows, :].reshape(8, 128, 256) * mrows[:, None, :]
                r = jnp.dot(
                    wv.reshape(1024, 256), GT[256 * w : 256 * (w + 1)],
                    preferred_element_type=F32,
                )
                acc = r if acc is None else acc + r
            acc = acc.astype(BF).reshape(4, 2, 128, 256)
            for cc in range(2):
                part[cc, yy, pl.ds(i * 4, 4)] = acc[:, cc]
            return carry

        lax.fori_loop(0, 2, step, 0)
        I[col] = Remote(part.at[1 - c, yy], crecv.at[yy], dev_sib)

    def core_sum(col):
        yy = cols[col]
        I[col].recv()
        for zz in range(NZ):
            v = part[c, yy, zz].astype(F32) + crecv[yy, zz].astype(F32)
            ysum[yy, zz] = v.astype(BF)

    def add(dst, src):
        dst[...] = (dst[...].astype(F32) + src[...].astype(F32)).astype(BF)

    def rs_first():
        R["A"] = Remote(ysum.at[yo, pl.ds(0, 4)], yrA, dev_yp)
        R["B"] = Remote(ysum.at[yo, pl.ds(4, 4)], yrB, dev_ym)

    def rs_second():
        R["A"].recv()
        for i in range(4):
            add(ysum.at[yp, i], yrA.at[i])
        R["m"] = Remote(ysum.at[yp], yr2m, dev_yp)
        R["B"].recv()
        for i in range(4):
            add(ysum.at[ym, 4 + i], yrB.at[i])
        R["p"] = Remote(ysum.at[ym], yr2p, dev_ym)

    def rs_z(step):
        if step == 4:
            R["m"].recv()
            R["p"].recv()
            for d in (4, 3, 5, 2, 6, 1, 7, 0):
                i = lax.rem(z + d, NZ)
                v = ysum[y, i].astype(F32) + yr2m[i].astype(F32) + yr2p[i].astype(F32)
                ysum[y, i] = v.astype(BF)
                if d == 4:
                    R["u", 4] = Remote(ysum.at[y, i, pl.ds(0, 64)], zra, dev_z(1))
                    R["d", 4] = Remote(ysum.at[y, i, pl.ds(64, 64)], zrb, dev_z(NZ - 1))
        elif step > 0:
            d = step
            for way, n, half, end in (("u", 0, zra, 1), ("d", 1, zrb, NZ - 1)):
                i = lax.rem(z + (d if n == 0 else NZ - d), NZ)
                R[way, d + 1].recv()
                if d == 3:
                    add(ysum.at[y, i, pl.ds(64 * n, 64)], half)
                else:
                    add(ysum.at[y, i], zr.at[n, 2 - d])
                R[way, d] = Remote(ysum.at[y, i], zr.at[n, 3 - d], dev_z(end))
        else:
            R["u", 1].recv()
            R["d", 1].recv()
            ig_ref[...] = ysum[y, z].astype(F32) + zr[0, 2].astype(F32) + zr[1, 2].astype(F32)

    def wgrad(h, g0=0, g1=4):
        for d in (1, 3, 2):
            X["g", d].recv()
        for (half, _), r in S.items():
            if half == h:
                r.recv()

        def group(gi, carry):
            for w in range(2):
                def gather(i, carry2):
                    k = lax.rem(m + gi * 16 + i, NM)
                    b = perm_ref[w, k]
                    cc = lax.rem(b, NC)
                    zz = lax.rem(lax.div(b, NC), NZ)
                    yy = lax.div(b, NC * NZ)
                    o = lax.rem(zz + NZ - z, NZ)
                    rows = pl.ds(pl.multiple_of(i * HALF, HALF), HALF)
                    if h == 0:
                        lhs[w, :, rows, :] = tt0[cc, yy, slot_of(o)]
                    else:
                        lhs[w, :, rows, :] = tt1[cc, slot_of(o), yy]
                    for j in range(2):
                        fs[w, j, rows, :] = jnp.broadcast_to(
                            facx[w, j, pl.ds(b, 1), :], (HALF, 128)
                        )
                    return carry2

                lax.fori_loop(0, 16, gather, 0, unroll=True)
                tot = None
                for p in range(NX):
                    r = jnp.dot(lhs[w, p], G[p, w], preferred_element_type=F32)
                    v = r[:, :128] * fs[w, 0] + r[:, 128:] * fs[w, 1]
                    v = jnp.clip(v, -1.0, 1.0).astype(BF).astype(F32)
                    tot = v if tot is None else tot + v
                abuf[h, pl.ds(gi * 16, 16), w] = tot.astype(BF).reshape(16, HALF, 128)

            def push(i, carry2):
                k = lax.rem(m + i, NM)

                @pl.when(i > 0)
                def _():
                    pltpu.make_async_remote_copy(
                        src_ref=abuf.at[h, i], dst_ref=recv_ref.at[h, m],
                        send_sem=a_ss.at[h], recv_sem=a_rs.at[h],
                        device_id=(q, k), device_id_type=MESH,
                    ).start()

                return carry2

            lax.fori_loop(gi * 16, gi * 16 + 16, push, 0)
            return carry

        lax.fori_loop(g0, g1, group, 0)
        if g0 == 0:
            cp = pltpu.make_async_copy(abuf.at[h, 0], recv_ref.at[h, m], lsem.at[6 + h])
            cp.start()
            own.append((h, cp))

    ops = {
        "xt": x_tokens, "zs": z_start, "y": y_first, "o": y_second, "b": sibling,
        "ys": y_start, "k": k_step, "bk": k_sibling,
        "ga": act_grads, "gx": x_grads, "mk": masks, "il": ig_load, "i": ig_chunk,
        "c": core_sum, "r1": rs_first, "r2": rs_second, "rz": rs_z, "w": wgrad,
    }
    for name, *args in SCHEDULE:
        ops[name](*args)

    for h, cp in own:
        cp.wait()
        done = pltpu.make_async_remote_copy(
            src_ref=abuf.at[h, pl.ds(1, NM - 1)], dst_ref=recv_ref.at[h, pl.ds(0, NM - 1)],
            send_sem=a_ss.at[h], recv_sem=a_rs.at[h], device_id=dev_sib, device_id_type=MESH,
        )
        done.wait_recv()
        done.wait_send()
    for r in sent:
        r.recv()
        r.copy.wait_send()


def expand(recv_ref, fac_ref, igt_ref, out_ref, ig_ref, rbuf, obuf, lsem, osem):
    n = 4
    per = NM // n
    ins = []
    for g in range(n):
        part = pl.ds(g * per, per)
        cp = pltpu.make_async_copy(recv_ref.at[:, part], rbuf.at[:, part], lsem.at[g])
        cp.start()
        ins.append(cp)
    ig_ref[...] = igt_ref[...].T.astype(BF)
    outs = []
    for g in range(n):
        ins[g].wait()
        for i in range(g * per, (g + 1) * per):
            for w in range(2):
                for h in range(2):
                    v = rbuf[h, i, w].astype(F32)
                    for j in range(2):
                        col = (i * 2 + j) * 128
                        f = fac_ref[w, i * 2 + j]
                        obuf[w, h * HALF : (h + 1) * HALF, col : col + 128] = v * f
        cols = pl.ds(g * per * 256, per * 256)
        cp = pltpu.make_async_copy(obuf.at[:, :, cols], out_ref.at[:, :, cols], osem.at[g])
        cp.start()
        outs.append(cp)
    for cp in outs:
        cp.wait()


def body(tokens, gate_act, up_act, hidden_grad, gate_weight, up_weight, block_mask, row_perm, scale_exp):
    any_spec = pl.BlockSpec(memory_space=pl.ANY)
    vm = pl.BlockSpec(memory_space=pltpu.VMEM)
    sm = pl.BlockSpec(memory_space=pltpu.SMEM)
    V = pltpu.VMEM
    igt, recv, fac = pl.pallas_call(
        kernel,
        out_shape=(
            jax.ShapeDtypeStruct((128, 256), F32),
            jax.ShapeDtypeStruct((2, NM, 2, HALF, 128), BF),
            jax.ShapeDtypeStruct((2, 128), F32),
        ),
        in_specs=[any_spec] * 6 + [vm, sm, vm],
        out_specs=(vm, any_spec, vm),
        scratch_shapes=[
            V((256, 128), BF), V((256, 256), BF), V((256, 256), BF), V((256, 256), BF),
            V((8192, 256), BF), V((8192, 256), BF),
            V((2, NX, HALF, 256), BF),
            V((2, NY, NZ, NX, HALF, 256), BF), V((2, NZ, NY, NX, HALF, 256), BF),
            V((NX, 2, 256, 256), BF), V((512, 256), BF),
            V((2, NM, 256), F32), V((2, 2, NM, 128), F32),
            V((2, NX, 256, 256), BF), V((2, 2, 256, 128), F32),
            V((2, NM, 2, HALF, 128), BF),
            V((2, NY, NZ, 128, 256), BF), V((NY, NZ, 128, 256), BF), V((NY, NZ, 128, 256), BF),
            V((4, 128, 256), BF), V((4, 128, 256), BF), V((NZ, 128, 256), BF), V((NZ, 128, 256), BF),
            V((64, 256), BF), V((64, 256), BF), V((2, 3, 128, 256), BF),
            pltpu.SemaphoreType.DMA((N_SEM,)), pltpu.SemaphoreType.DMA((N_SEM,)),
            pltpu.SemaphoreType.DMA((2,)), pltpu.SemaphoreType.DMA((2,)),
            pltpu.SemaphoreType.DMA((8,)),
        ],
        compiler_params=pltpu.CompilerParams(
            collective_id=0, has_side_effects=True, vmem_limit_bytes=56 << 20
        ),
        name="grads",
    )(tokens, gate_act, up_act, hidden_grad, gate_weight, up_weight, block_mask, row_perm, scale_exp)
    out, ig = pl.pallas_call(
        expand,
        out_shape=(
            jax.ShapeDtypeStruct((2, 32, 16384), F32),
            jax.ShapeDtypeStruct((256, 128), BF),
        ),
        in_specs=[any_spec, sm, vm],
        out_specs=(any_spec, vm),
        scratch_shapes=[
            V((2, NM, 2, HALF, 128), BF), V((2, 32, 16384), F32),
            pltpu.SemaphoreType.DMA((4,)), pltpu.SemaphoreType.DMA((4,)),
        ],
        compiler_params=pltpu.CompilerParams(vmem_limit_bytes=32 << 20),
        name="expand",
    )(recv, fac, igt)
    return ig, out


def solution(mesh):
    act = P("dp", "mp")
    weight = P(None, "mp")
    in_specs = (act, act, act, act, weight, weight, P(), P(), P())
    out_specs = (act, P(None, ("mp", "dp"), None))
    return jax.shard_map(body, mesh=mesh, in_specs=in_specs, out_specs=out_specs, check_vma=False)
```

```python
import jax
import jax.numpy as jnp
from jax import lax
from jax.experimental import pallas as pl
from jax.experimental.pallas import tpu as pltpu
from jax.sharding import PartitionSpec as P

BF = jnp.bfloat16
F32 = jnp.float32
MESH = pl.DeviceIdType.MESH
NX, NY, NZ, NC = 4, 4, 8, 2
NM = NY * NZ * NC
HALF = 16
N_SEM = 96


def slot_of(o):
    return jnp.where(o <= 3, 2 * o, jnp.where(o == 4, 7, 2 * (8 - o) - 1))


def static_slot(o):
    o %= 8
    return 2 * o if o <= 3 else (7 if o == 4 else 2 * (8 - o) - 1)


SCHEDULE = (
    ("xt",), ("ga",), ("mk",), ("il",), ("i", "o"), ("i", "p"), ("i", "m"), ("i", "s"), ("zs",),
    ("y", 0), ("ys",), ("gx",), ("c", "o"), ("r1",), ("y", 1), ("k", 1), ("bk", 0), ("o", 0),
    ("y", 2), ("b", "s"), ("c", "p"), ("c", "m"), ("c", "s"), ("k", 2), ("bk", 1), ("o", 1),
    ("o", 2), ("k", 3), ("bk", 2), ("r2",), ("b", "m"), ("b", "p"), ("k", 4), ("bk", 3), ("b", "o"),
    ("w", 0), ("bk", 4), ("w", 1, 0, 1), ("rz", 4), ("w", 1, 1, 2), ("rz", 3), ("w", 1, 2, 3),
    ("rz", 2), ("w", 1, 3, 4), ("rz", 1), ("rz", 0),
)


def kernel(
    tok_ref, g_ref, u_ref, h_ref, wg_ref, wu_ref, mask_hbm, perm_hbm, exp_hbm,
    ig_ref, recv_ref, fac_ref,
    mask_ref, perm_ref, exp_ref,
    tok, gact, uact, hgrad, wg, wu, xsrc, tt0, tt1, G, GT, wm, facx, lhs, fs, abuf,
    part, crecv, ysum, yrA, yrB, yr2m, yr2p, zra, zrb, zr, zd,
    ss, rs, a_ss, a_rs, lsem,
):
    q = lax.axis_index("dp")
    m = lax.axis_index("mp")
    c = lax.rem(m, NC)
    z = lax.rem(lax.div(m, NC), NZ)
    y = lax.div(m, NC * NZ)
    yp, ym, yo = lax.rem(y + 1, NY), lax.rem(y + 3, NY), lax.rem(y + 2, NY)

    def mp_of(yy, zz, cc):
        return (yy * NZ + zz) * NC + cc

    dev_yp, dev_ym = (q, mp_of(yp, z, c)), (q, mp_of(ym, z, c))
    dev_sib = (q, mp_of(y, z, 1 - c))

    def dev_z(d):
        return (q, mp_of(y, lax.rem(z + d, NZ), c))

    def dev_x(d):
        return (lax.rem(q + d, NX), m)

    loads = []
    for i, (src, dst) in enumerate(
        ((tok_ref, tok), (g_ref, gact), (u_ref, uact), (h_ref, hgrad))
    ):
        cp = pltpu.make_async_copy(src, dst, lsem.at[i])
        cp.start()
        loads.append(cp)
    for i, (src, dst) in enumerate(
        ((mask_hbm, mask_ref), (perm_hbm, perm_ref), (exp_hbm, exp_ref))
    ):
        cp = pltpu.make_async_copy(src, dst, lsem.at[8 + i])
        cp.start()
        loads.append(cp)
    wloads = []
    for i, (src, dst) in enumerate(((wg_ref, wg), (wu_ref, wu))):
        cp = pltpu.make_async_copy(src, dst, lsem.at[4 + i])
        cp.start()
        wloads.append(cp)

    barrier = pltpu.get_barrier_semaphore()

    partners = [dev_sib] + [dev_z(d) for d in range(1, NZ)] + [dev_x(d) for d in range(1, NX)]
    partners += [(q, mp_of(lax.rem(y + d, NY), z, c)) for d in range(1, NY)]
    for dev in partners:
        pl.semaphore_signal(barrier, inc=1, device_id=dev, device_id_type=MESH)

    sent = []

    class Remote:
        def __init__(self, src, dst, dev):
            i = len(sent)
            self.copy = pltpu.make_async_remote_copy(
                src_ref=src, dst_ref=dst, send_sem=ss.at[i], recv_sem=rs.at[i],
                device_id=dev, device_id_type=MESH,
            )
            self.copy.start()
            self.pending = True
            sent.append(self)

        def recv(self):
            if self.pending:
                self.copy.wait_recv()
                self.pending = False

    X, Z, Y, O, K, S, I, R = ({} for _ in range(8))
    own = []
    cols = {"s": y, "p": yp, "m": ym, "o": yo}

    def own_block(h):
        return tt0.at[c, y, 0] if h == 0 else tt1.at[c, 0, y]

    def x_tokens():
        loads[0].wait()
        tok_t = tok[...].T
        for h in range(2):
            for k in range(NX):
                xsrc[h, k] = tok_t[32 * k + HALF * h : 32 * k + HALF * (h + 1), :]
            own_block(h)[q] = xsrc[h, q]
        pl.semaphore_wait(barrier, len(partners))
        for h in range(2):
            for d in (1, 3, 2):
                to = lax.rem(q + d, NX)
                X[h, d] = Remote(xsrc.at[h, to], own_block(h).at[q], dev_x(d))

    def z_start():
        for d in (1, 3, 2):
            X[0, d].recv()
        for d in (1, 7, 2, 6, 3, 5, 4):
            Z[d] = Remote(tt0.at[c, y, 0], tt0.at[c, y, static_slot(-d)], dev_z(d))

    groups = ((0, 1, ()), (1, 3, (1, 7)), (3, 8, (2, 6, 3, 5, 4)))

    def y_first(g):
        s0, s1, ds = groups[g]
        for d in ds:
            Z[d].recv()
        r = tt0.at[c, y, pl.ds(s0, s1 - s0)]
        Y[g, "m"] = Remote(r, r, dev_yp)
        Y[g, "p"] = Remote(r, r, dev_ym)

    def y_direct(g):
        y_first(g)
        s0, s1, _ = groups[g]
        r = tt0.at[c, y, pl.ds(s0, s1 - s0)]
        O[g, 0] = Remote(r, r, (q, mp_of(yo, z, c)))
        O[g, 1] = O[g, 0]

    def y_second(g):
        s0, s1, _ = groups[g]
        Y[g, "m"].recv()
        r = tt0.at[c, ym, pl.ds(s0, s1 - s0), pl.ds(0, 2)]
        O[g, 0] = Remote(r, r, dev_yp)
        Y[g, "p"].recv()
        r = tt0.at[c, yp, pl.ds(s0, s1 - s0), pl.ds(2, 2)]
        O[g, 1] = Remote(r, r, dev_ym)

    def sibling(col):
        for g in range(3):
            if col == "o":
                O[g, 0].recv()
                O[g, 1].recv()
            elif col != "s":
                Y[g, col].recv()
        r = tt0.at[c, cols[col]]
        S[0, col] = Remote(r, r, dev_sib)

    def y_start():
        for d in (1, 3, 2):
            X[1, d].recv()
        r = own_block(1)
        for d in (1, 3, 2):
            Y["k", d] = Remote(r, r, (q, mp_of(lax.rem(y + d, NY), z, c)))

    def k_recv(step):
        for way in (1, -1):
            for n in range(2):
                if (step, way, n) in K:
                    K[step, way, n].recv()

    def k_step(step):
        if step == 1:
            for d in (1, 3, 2):
                Y["k", d].recv()
        for n in range(2):
            for way in (1, -1):
                if step == 4 and (way == 1) != (n == 0):
                    continue
                if step > 1:
                    K[step - 1, way, n].recv()
                half = pl.ds(2 * n, 2)
                src = tt1.at[c, static_slot(-way * (step - 1)), half]
                dst = tt1.at[c, static_slot(-way * step), half]
                K[step, way, n] = Remote(src, dst, dev_z(way % NZ))

    def k_sibling(g):
        k_recv(g)
        s0, s1 = ((0, 1), (1, 3), (3, 5), (5, 7), (7, 8))[g]
        r = tt1.at[c, pl.ds(s0, s1 - s0)]
        S[1, g] = Remote(r, r, dev_sib)

    def act_grads():
        for cp in loads[1:4]:
            cp.wait()
        gf = gact[...].astype(F32)
        hf = hgrad[...].astype(F32)
        sig = jax.nn.sigmoid(gf)
        gg = (hf * uact[...].astype(F32) * sig * (1.0 + gf * (1.0 - sig))).astype(BF)
        ug = (hf * gf * sig).astype(BF)
        G[q, 0] = gg
        G[q, 1] = ug
        GT[0:256] = gg.T
        GT[256:512] = ug.T

    def x_grads():
        for d in (1, 3, 2):
            X["g", d] = Remote(G.at[q], G.at[q], dev_x(d))

    def masks():
        for cp in loads[4:]:
            cp.wait()
        lane = lax.broadcasted_iota(jnp.int32, (2, NM, 128), 2)
        for j in range(2):
            pick = lane == 2 * m + j
            mk = jnp.sum(jnp.where(pick, mask_ref[...], 0).astype(F32), axis=2, keepdims=True)
            ex = jnp.sum(jnp.where(pick, exp_ref[...], 0).astype(F32), axis=2, keepdims=True)
            mkb = jnp.broadcast_to(mk, (2, NM, 128))
            facx[:, j] = mkb * jnp.exp2(-jnp.broadcast_to(ex, (2, NM, 128)))
            wm[:, :, 128 * j : 128 * (j + 1)] = mkb
        for w in range(2):
            row = perm_ref[w, m]
            mrow = mask_ref[w, pl.ds(row, 1), :].astype(F32)
            erow = exp_ref[w, pl.ds(row, 1), :].astype(F32)
            fac_ref[w] = jnp.broadcast_to(mrow * jnp.exp2(erow), (128, 128)).T

    def ig_load():
        for cp in wloads:
            cp.wait()

    def ig_chunk(col):
        yy = cols[col]

        def step(i, carry):
            blk = yy * 16 + i * 8
            rows = pl.ds(pl.multiple_of(blk * 128, 1024), 1024)
            acc = None
            for w, wref in enumerate((wg, wu)):
                mrows = wm[w, pl.ds(pl.multiple_of(blk, 8), 8), :].astype(BF)
                wv = wref[rows, :].reshape(8, 128, 256) * mrows[:, None, :]
                r = jnp.dot(
                    wv.reshape(1024, 256), GT[256 * w : 256 * (w + 1)],
                    preferred_element_type=F32,
                )
                acc = r if acc is None else acc + r
            acc = acc.astype(BF).reshape(4, 2, 128, 256)
            for cc in range(2):
                part[cc, yy, pl.ds(i * 4, 4)] = acc[:, cc]
            return carry

        lax.fori_loop(0, 2, step, 0)
        I[col] = Remote(part.at[1 - c, yy], crecv.at[yy], dev_sib)

    def core_sum(col):
        yy = cols[col]
        I[col].recv()
        for zz in range(NZ):
            v = part[c, yy, zz].astype(F32) + crecv[yy, zz].astype(F32)
            ysum[yy, zz] = v.astype(BF)

    def add(dst, src):
        dst[...] = (dst[...].astype(F32) + src[...].astype(F32)).astype(BF)

    def rs_first():
        R["A"] = Remote(ysum.at[yo, pl.ds(0, 4)], yrA, dev_yp)
        R["B"] = Remote(ysum.at[yo, pl.ds(4, 4)], yrB, dev_ym)

    def rs_early():
        R["eu"] = Remote(ysum.at[yp, pl.ds(4, 4)], yr2m.at[pl.ds(4, 4)], dev_yp)
        R["ed"] = Remote(ysum.at[ym, pl.ds(0, 4)], yr2p.at[pl.ds(0, 4)], dev_ym)

    def rs_second():
        R["A"].recv()
        for i in range(4):
            add(ysum.at[yp, i], yrA.at[i])
        up, down = (pl.ds(0, 4), pl.ds(4, 4)) if "eu" in R else (pl.ds(0, 8), pl.ds(0, 8))
        R["m"] = Remote(ysum.at[yp, up], yr2m.at[up], dev_yp)
        R["B"].recv()
        for i in range(4):
            add(ysum.at[ym, 4 + i], yrB.at[i])
        R["p"] = Remote(ysum.at[ym, down], yr2p.at[down], dev_ym)

    def rs_z_direct():
        for r in ("eu", "ed", "m", "p"):
            if r in R:
                R[r].recv()
        for d in (4, 3, 5, 2, 6, 1, 7, 0):
            i = lax.rem(z + d, NZ)
            v = ysum[y, i].astype(F32) + yr2m[i].astype(F32) + yr2p[i].astype(F32)
            if d == 0:
                ig_ref[...] = v
            else:
                ysum[y, i] = v.astype(BF)
                R["z", d] = Remote(ysum.at[y, i], zd.at[d - 1], dev_z(d))

    def rs_final():
        for d in range(1, NZ):
            R["z", d].recv()
        v = ig_ref[...]
        for d in range(1, NZ):
            v = v + zd[d - 1].astype(F32)
        ig_ref[...] = v

    def rs_z(step):
        if step == 4:
            for r in ("eu", "ed", "m", "p"):
                if r in R:
                    R[r].recv()
            for d in (4, 3, 5, 2, 6, 1, 7, 0):
                i = lax.rem(z + d, NZ)
                v = ysum[y, i].astype(F32) + yr2m[i].astype(F32) + yr2p[i].astype(F32)
                ysum[y, i] = v.astype(BF)
                if d == 4:
                    R["u", 4] = Remote(ysum.at[y, i, pl.ds(0, 64)], zra, dev_z(1))
                    R["d", 4] = Remote(ysum.at[y, i, pl.ds(64, 64)], zrb, dev_z(NZ - 1))
        elif step > 0:
            d = step
            for way, n, half, end in (("u", 0, zra, 1), ("d", 1, zrb, NZ - 1)):
                i = lax.rem(z + (d if n == 0 else NZ - d), NZ)
                R[way, d + 1].recv()
                if d == 3:
                    add(ysum.at[y, i, pl.ds(64 * n, 64)], half)
                else:
                    add(ysum.at[y, i], zr.at[n, 2 - d])
                R[way, d] = Remote(ysum.at[y, i], zr.at[n, 3 - d], dev_z(end))
        else:
            R["u", 1].recv()
            R["d", 1].recv()
            ig_ref[...] = ysum[y, z].astype(F32) + zr[0, 2].astype(F32) + zr[1, 2].astype(F32)

    def wgrad(h, g0=0, g1=4):
        for d in (1, 3, 2):
            X["g", d].recv()
        for (half, _), r in S.items():
            if half == h:
                r.recv()

        def group(gi, carry):
            for w in range(2):
                def gather(i, carry2):
                    k = lax.rem(m + gi * 16 + i, NM)
                    b = perm_ref[w, k]
                    cc = lax.rem(b, NC)
                    zz = lax.rem(lax.div(b, NC), NZ)
                    yy = lax.div(b, NC * NZ)
                    o = lax.rem(zz + NZ - z, NZ)
                    rows = pl.ds(pl.multiple_of(i * HALF, HALF), HALF)
                    if h == 0:
                        lhs[w, :, rows, :] = tt0[cc, yy, slot_of(o)]
                    else:
                        lhs[w, :, rows, :] = tt1[cc, slot_of(o), yy]
                    for j in range(2):
                        fs[w, j, rows, :] = jnp.broadcast_to(
                            facx[w, j, pl.ds(b, 1), :], (HALF, 128)
                        )
                    return carry2

                lax.fori_loop(0, 16, gather, 0, unroll=True)
                tot = None
                for p in range(NX):
                    r = jnp.dot(lhs[w, p], G[p, w], preferred_element_type=F32)
                    v = r[:, :128] * fs[w, 0] + r[:, 128:] * fs[w, 1]
                    v = jnp.clip(v, -1.0, 1.0).astype(BF).astype(F32)
                    tot = v if tot is None else tot + v
                abuf[h, pl.ds(gi * 16, 16), w] = tot.astype(BF).reshape(16, HALF, 128)

            def push(i, carry2):
                k = lax.rem(m + i, NM)

                @pl.when(i > 0)
                def _():
                    pltpu.make_async_remote_copy(
                        src_ref=abuf.at[h, i], dst_ref=recv_ref.at[h, m],
                        send_sem=a_ss.at[h], recv_sem=a_rs.at[h],
                        device_id=(q, k), device_id_type=MESH,
                    ).start()

                return carry2

            lax.fori_loop(gi * 16, gi * 16 + 16, push, 0)
            return carry

        lax.fori_loop(g0, g1, group, 0)
        if g0 == 0:
            cp = pltpu.make_async_copy(abuf.at[h, 0], recv_ref.at[h, m], lsem.at[6 + h])
            cp.start()
            own.append((h, cp))

    ops = {
        "xt": x_tokens, "zs": z_start, "y": y_first, "o": y_second, "yd": y_direct, "b": sibling,
        "ys": y_start, "k": k_step, "bk": k_sibling,
        "ga": act_grads, "gx": x_grads, "mk": masks, "il": ig_load, "i": ig_chunk,
        "c": core_sum, "r1": rs_first, "re": rs_early, "r2": rs_second,
        "rd": rs_z_direct, "rf": rs_final, "rz": rs_z, "w": wgrad,
    }
    for name, *args in SCHEDULE:
        ops[name](*args)

    for h, cp in own:
        cp.wait()
        done = pltpu.make_async_remote_copy(
            src_ref=abuf.at[h, pl.ds(1, NM - 1)], dst_ref=recv_ref.at[h, pl.ds(0, NM - 1)],
            send_sem=a_ss.at[h], recv_sem=a_rs.at[h], device_id=dev_sib, device_id_type=MESH,
        )
        done.wait_recv()
        done.wait_send()
    for r in sent:
        r.recv()
        r.copy.wait_send()


def expand(recv_ref, fac_ref, igt_ref, out_ref, ig_ref, rbuf, obuf, lsem, osem):
    n = 4
    per = NM // n
    ins = []
    for g in range(n):
        part = pl.ds(g * per, per)
        cp = pltpu.make_async_copy(recv_ref.at[:, part], rbuf.at[:, part], lsem.at[g])
        cp.start()
        ins.append(cp)
    ig_ref[...] = igt_ref[...].T.astype(BF)
    outs = []
    for g in range(n):
        ins[g].wait()
        for i in range(g * per, (g + 1) * per):
            for w in range(2):
                for h in range(2):
                    v = rbuf[h, i, w].astype(F32)
                    for j in range(2):
                        col = (i * 2 + j) * 128
                        f = fac_ref[w, i * 2 + j : i * 2 + j + 1, :]
                        obuf[w, h * HALF : (h + 1) * HALF, col : col + 128] = v * f
        cols = pl.ds(g * per * 256, per * 256)
        cp = pltpu.make_async_copy(obuf.at[:, :, cols], out_ref.at[:, :, cols], osem.at[g])
        cp.start()
        outs.append(cp)
    for cp in outs:
        cp.wait()


def body(tokens, gate_act, up_act, hidden_grad, gate_weight, up_weight, block_mask, row_perm, scale_exp):
    any_spec = pl.BlockSpec(memory_space=pl.ANY)
    vm = pl.BlockSpec(memory_space=pltpu.VMEM)
    V = pltpu.VMEM
    igt, recv, fac = pl.pallas_call(
        kernel,
        out_shape=(
            V((128, 256), F32),
            V((2, NM, 2, HALF, 128), BF),
            V((2, 128, 128), F32),
        ),
        in_specs=[any_spec] * 9,
        out_specs=(vm, any_spec, vm),
        scratch_shapes=[
            V((2, NM, 128), jnp.int32), pltpu.SMEM((2, NM), jnp.int32), V((2, NM, 128), jnp.int32),
            V((256, 128), BF), V((256, 256), BF), V((256, 256), BF), V((256, 256), BF),
            V((8192, 256), BF), V((8192, 256), BF),
            V((2, NX, HALF, 256), BF),
            V((2, NY, NZ, NX, HALF, 256), BF), V((2, NZ, NY, NX, HALF, 256), BF),
            V((NX, 2, 256, 256), BF), V((512, 256), BF),
            V((2, NM, 256), F32), V((2, 2, NM, 128), F32),
            V((2, NX, 256, 256), BF), V((2, 2, 256, 128), F32),
            V((2, NM, 2, HALF, 128), BF),
            V((2, NY, NZ, 128, 256), BF), V((NY, NZ, 128, 256), BF), V((NY, NZ, 128, 256), BF),
            V((4, 128, 256), BF), V((4, 128, 256), BF), V((NZ, 128, 256), BF), V((NZ, 128, 256), BF),
            V((64, 256), BF), V((64, 256), BF), V((2, 3, 128, 256), BF),
            V((NZ - 1, 128, 256), BF),
            pltpu.SemaphoreType.DMA((N_SEM,)), pltpu.SemaphoreType.DMA((N_SEM,)),
            pltpu.SemaphoreType.DMA((2,)), pltpu.SemaphoreType.DMA((2,)),
            pltpu.SemaphoreType.DMA((11,)),
        ],
        compiler_params=pltpu.CompilerParams(
            collective_id=0, has_side_effects=True, vmem_limit_bytes=56 << 20
        ),
        name="grads",
    )(tokens, gate_act, up_act, hidden_grad, gate_weight, up_weight, block_mask, row_perm, scale_exp)
    out, ig = pl.pallas_call(
        expand,
        out_shape=(
            jax.ShapeDtypeStruct((2, 32, 16384), F32),
            jax.ShapeDtypeStruct((256, 128), BF),
        ),
        in_specs=[any_spec, vm, vm],
        out_specs=(any_spec, vm),
        scratch_shapes=[
            V((2, NM, 2, HALF, 128), BF), V((2, 32, 16384), F32),
            pltpu.SemaphoreType.DMA((4,)), pltpu.SemaphoreType.DMA((4,)),
        ],
        compiler_params=pltpu.CompilerParams(vmem_limit_bytes=32 << 20),
        name="expand",
    )(recv, fac, igt)
    return ig, out


def solution(mesh):
    act = P("dp", "mp")
    weight = P(None, "mp")
    in_specs = (act, act, act, act, weight, weight, P(), P(), P())
    out_specs = (act, P(None, ("mp", "dp"), None))
    return jax.shard_map(body, mesh=mesh, in_specs=in_specs, out_specs=out_specs, check_vma=False)
```

```python
import jax
import jax.numpy as jnp
from jax import lax
from jax.experimental import pallas as pl
from jax.experimental.pallas import tpu as pltpu
from jax.sharding import PartitionSpec as P

BF = jnp.bfloat16
F32 = jnp.float32
MESH = pl.DeviceIdType.MESH
NX, NY, NZ, NC = 4, 4, 8, 2
NM = NY * NZ * NC
HALF = 16
N_SEM = 96


def slot_of(o):
    return jnp.where(o <= 3, 2 * o, jnp.where(o == 4, 7, 2 * (8 - o) - 1))


def static_slot(o):
    o %= 8
    return 2 * o if o <= 3 else (7 if o == 4 else 2 * (8 - o) - 1)


SCHEDULE = (
    ("xt",), ("ga",), ("gx",), ("mk",), ("il",), ("i", "o"), ("i", "p"), ("i", "m"), ("i", "s"),
    ("zs",), ("y", 0), ("ys",), ("c", "o"), ("r1",), ("y", 1), ("k", 1), ("bk", 0), ("o", 0),
    ("y", 2), ("c", "p"), ("c", "m"), ("c", "s"), ("k", 2), ("bk", 1), ("o", 1), ("y", 3),
    ("b", "s"), ("o", 2), ("k", 3), ("bk", 2), ("o", 3), ("r2",), ("b", "m"), ("b", "p"), ("k", 4),
    ("bk", 3), ("b", "o"), ("w", 0), ("bk", 4), ("w", 1, 0, 1), ("rz", 4), ("w", 1, 1, 2),
    ("rz", 3), ("w", 1, 2, 3), ("rz", 2), ("w", 1, 3, 4), ("rz", 1), ("rz", 0),
)


def kernel(
    tok_ref, g_ref, u_ref, h_ref, wg_ref, wu_ref, mask_hbm, perm_hbm, exp_hbm,
    ig_ref, recv_ref, fac_ref,
    mask_ref, perm_ref, exp_ref,
    tok, gact, uact, hgrad, wg, wu, xsrc, tt0, tt1, G, GT, wm, facx, lhs, fs, abuf,
    part, crecv, ysum, yrA, yrB, yr2m, yr2p, zra, zrb, zr,
    ss, rs, a_ss, a_rs, lsem,
):
    q = lax.axis_index("dp")
    m = lax.axis_index("mp")
    c = lax.rem(m, NC)
    z = lax.rem(lax.div(m, NC), NZ)
    y = lax.div(m, NC * NZ)
    yp, ym, yo = lax.rem(y + 1, NY), lax.rem(y + 3, NY), lax.rem(y + 2, NY)

    def mp_of(yy, zz, cc):
        return (yy * NZ + zz) * NC + cc

    dev_yp, dev_ym = (q, mp_of(yp, z, c)), (q, mp_of(ym, z, c))
    dev_sib = (q, mp_of(y, z, 1 - c))

    def dev_z(d):
        return (q, mp_of(y, lax.rem(z + d, NZ), c))

    def dev_x(d):
        return (lax.rem(q + d, NX), m)

    loads = []
    for i, (src, dst) in enumerate(
        ((tok_ref, tok), (g_ref, gact), (u_ref, uact), (h_ref, hgrad))
    ):
        cp = pltpu.make_async_copy(src, dst, lsem.at[i])
        cp.start()
        loads.append(cp)
    for i, (src, dst) in enumerate(
        ((mask_hbm, mask_ref), (perm_hbm, perm_ref), (exp_hbm, exp_ref))
    ):
        cp = pltpu.make_async_copy(src, dst, lsem.at[8 + i])
        cp.start()
        loads.append(cp)
    wloads = []
    for i, (src, dst) in enumerate(((wg_ref, wg), (wu_ref, wu))):
        cp = pltpu.make_async_copy(src, dst, lsem.at[4 + i])
        cp.start()
        wloads.append(cp)

    barrier = pltpu.get_barrier_semaphore()

    partners = [dev_sib] + [dev_z(d) for d in range(1, NZ)] + [dev_x(d) for d in range(1, NX)]
    partners += [(q, mp_of(lax.rem(y + d, NY), z, c)) for d in range(1, NY)]
    for dev in partners:
        pl.semaphore_signal(barrier, inc=1, device_id=dev, device_id_type=MESH)

    sent = []

    class Remote:
        def __init__(self, src, dst, dev):
            i = len(sent)
            self.copy = pltpu.make_async_remote_copy(
                src_ref=src, dst_ref=dst, send_sem=ss.at[i], recv_sem=rs.at[i],
                device_id=dev, device_id_type=MESH,
            )
            self.copy.start()
            self.pending = True
            sent.append(self)

        def recv(self):
            if self.pending:
                self.copy.wait_recv()
                self.pending = False

    X, Z, Y, O, K, S, I, R = ({} for _ in range(8))
    own = []
    cols = {"s": y, "p": yp, "m": ym, "o": yo}

    def own_block(h):
        return tt0.at[c, y, 0] if h == 0 else tt1.at[c, 0, y]

    def x_tokens():
        loads[0].wait()
        tok_t = tok[...].T
        for h in range(2):
            for k in range(NX):
                xsrc[h, k] = tok_t[32 * k + HALF * h : 32 * k + HALF * (h + 1), :]
            own_block(h)[q] = xsrc[h, q]
        pl.semaphore_wait(barrier, len(partners))
        for h in range(2):
            for d in (1, 3, 2):
                to = lax.rem(q + d, NX)
                X[h, d] = Remote(xsrc.at[h, to], own_block(h).at[q], dev_x(d))

    def z_start():
        for d in (1, 3, 2):
            X[0, d].recv()
        for d in (1, 7, 2, 6, 3, 5, 4):
            Z[d] = Remote(tt0.at[c, y, 0], tt0.at[c, y, static_slot(-d)], dev_z(d))

    groups = ((0, 1, ()), (1, 3, (1, 7)), (3, 5, (2, 6)), (5, 8, (3, 5, 4)))

    def y_first(g):
        s0, s1, ds = groups[g]
        for d in ds:
            Z[d].recv()
        r = tt0.at[c, y, pl.ds(s0, s1 - s0)]
        Y[g, "m"] = Remote(r, r, dev_yp)
        Y[g, "p"] = Remote(r, r, dev_ym)

    def y_second(g):
        s0, s1, _ = groups[g]
        Y[g, "m"].recv()
        r = tt0.at[c, ym, pl.ds(s0, s1 - s0), pl.ds(0, 2)]
        O[g, 0] = Remote(r, r, dev_yp)
        Y[g, "p"].recv()
        r = tt0.at[c, yp, pl.ds(s0, s1 - s0), pl.ds(2, 2)]
        O[g, 1] = Remote(r, r, dev_ym)

    def sibling(col, g0=0, g1=4):
        for g in range(g0, g1):
            if col == "o":
                O[g, 0].recv()
                O[g, 1].recv()
            elif col == "s":
                for d in groups[g][2]:
                    Z[d].recv()
            else:
                Y[g, col].recv()
        s0, s1 = groups[g0][0], groups[g1 - 1][1]
        r = tt0.at[c, cols[col], pl.ds(s0, s1 - s0)]
        S[0, (col, g0)] = Remote(r, r, dev_sib)

    def y_start():
        for d in (1, 3, 2):
            X[1, d].recv()
        r = own_block(1)
        for d in (1, 3, 2):
            Y["k", d] = Remote(r, r, (q, mp_of(lax.rem(y + d, NY), z, c)))

    def k_recv(step):
        for way in (1, -1):
            for n in range(2):
                if (step, way, n) in K:
                    K[step, way, n].recv()

    def k_step(step):
        if step == 1:
            for d in (1, 3, 2):
                Y["k", d].recv()
        for n in range(2):
            for way in (1, -1):
                if step == 4 and (way == 1) != (n == 0):
                    continue
                if step > 1:
                    K[step - 1, way, n].recv()
                half = pl.ds(2 * n, 2)
                src = tt1.at[c, static_slot(-way * (step - 1)), half]
                dst = tt1.at[c, static_slot(-way * step), half]
                K[step, way, n] = Remote(src, dst, dev_z(way % NZ))

    def k_sibling(g):
        k_recv(g)
        s0, s1 = ((0, 1), (1, 3), (3, 5), (5, 7), (7, 8))[g]
        r = tt1.at[c, pl.ds(s0, s1 - s0)]
        S[1, g] = Remote(r, r, dev_sib)

    def act_grads():
        for cp in loads[1:4]:
            cp.wait()
        gf = gact[...].astype(F32)
        hf = hgrad[...].astype(F32)
        sig = jax.nn.sigmoid(gf)
        gg = (hf * uact[...].astype(F32) * sig * (1.0 + gf * (1.0 - sig))).astype(BF)
        ug = (hf * gf * sig).astype(BF)
        G[q, 0] = gg
        G[q, 1] = ug
        GT[0:256] = gg.T
        GT[256:512] = ug.T

    def x_grads():
        for d in (1, 3, 2):
            X["g", d] = Remote(G.at[q], G.at[q], dev_x(d))

    def masks():
        for cp in loads[4:]:
            cp.wait()
        lane = lax.broadcasted_iota(jnp.int32, (2, NM, 128), 2)
        for j in range(2):
            pick = lane == 2 * m + j
            mk = jnp.sum(jnp.where(pick, mask_ref[...], 0).astype(F32), axis=2, keepdims=True)
            ex = jnp.sum(jnp.where(pick, exp_ref[...], 0).astype(F32), axis=2, keepdims=True)
            mkb = jnp.broadcast_to(mk, (2, NM, 128))
            facx[:, j] = mkb * jnp.exp2(-jnp.broadcast_to(ex, (2, NM, 128)))
            wm[:, :, 128 * j : 128 * (j + 1)] = mkb
        for w in range(2):
            row = perm_ref[w, m]
            mrow = mask_ref[w, pl.ds(row, 1), :].astype(F32)
            erow = exp_ref[w, pl.ds(row, 1), :].astype(F32)
            fac_ref[w] = jnp.broadcast_to(mrow * jnp.exp2(erow), (128, 128)).T

    def ig_load():
        for cp in wloads:
            cp.wait()

    def ig_chunk(col):
        yy = cols[col]

        def step(i, carry):
            blk = yy * 16 + i * 8
            rows = pl.ds(pl.multiple_of(blk * 128, 1024), 1024)
            acc = None
            for w, wref in enumerate((wg, wu)):
                mrows = wm[w, pl.ds(pl.multiple_of(blk, 8), 8), :].astype(BF)
                wv = wref[rows, :].reshape(8, 128, 256) * mrows[:, None, :]
                r = jnp.dot(
                    wv.reshape(1024, 256), GT[256 * w : 256 * (w + 1)],
                    preferred_element_type=F32,
                )
                acc = r if acc is None else acc + r
            acc = acc.astype(BF).reshape(4, 2, 128, 256)
            for cc in range(2):
                part[cc, yy, pl.ds(i * 4, 4)] = acc[:, cc]
            return carry

        lax.fori_loop(0, 2, step, 0)
        I[col] = Remote(part.at[1 - c, yy], crecv.at[yy], dev_sib)

    def core_sum(col):
        yy = cols[col]
        I[col].recv()
        for zz in range(NZ):
            v = part[c, yy, zz].astype(F32) + crecv[yy, zz].astype(F32)
            ysum[yy, zz] = v.astype(BF)

    def add(dst, src):
        dst[...] = (dst[...].astype(F32) + src[...].astype(F32)).astype(BF)

    def rs_first():
        R["A"] = Remote(ysum.at[yo, pl.ds(0, 4)], yrA, dev_yp)
        R["B"] = Remote(ysum.at[yo, pl.ds(4, 4)], yrB, dev_ym)

    def rs_second():
        R["A"].recv()
        for i in range(4):
            add(ysum.at[yp, i], yrA.at[i])
        R["m"] = Remote(ysum.at[yp], yr2m, dev_yp)
        R["B"].recv()
        for i in range(4):
            add(ysum.at[ym, 4 + i], yrB.at[i])
        R["p"] = Remote(ysum.at[ym], yr2p, dev_ym)

    def rs_z(step):
        if step == 4:
            R["m"].recv()
            R["p"].recv()
            for d in (4, 3, 5, 2, 6, 1, 7, 0):
                i = lax.rem(z + d, NZ)
                v = ysum[y, i].astype(F32) + yr2m[i].astype(F32) + yr2p[i].astype(F32)
                ysum[y, i] = v.astype(BF)
                if d == 4:
                    R["u", 4] = Remote(ysum.at[y, i, pl.ds(0, 64)], zra, dev_z(1))
                    R["d", 4] = Remote(ysum.at[y, i, pl.ds(64, 64)], zrb, dev_z(NZ - 1))
        elif step > 0:
            d = step
            for way, n, half, end in (("u", 0, zra, 1), ("d", 1, zrb, NZ - 1)):
                i = lax.rem(z + (d if n == 0 else NZ - d), NZ)
                R[way, d + 1].recv()
                if d == 3:
                    add(ysum.at[y, i, pl.ds(64 * n, 64)], half)
                else:
                    add(ysum.at[y, i], zr.at[n, 2 - d])
                R[way, d] = Remote(ysum.at[y, i], zr.at[n, 3 - d], dev_z(end))
        else:
            R["u", 1].recv()
            R["d", 1].recv()
            ig_ref[...] = ysum[y, z].astype(F32) + zr[0, 2].astype(F32) + zr[1, 2].astype(F32)

    def wgrad(h, g0=0, g1=4):
        for d in (1, 3, 2):
            X["g", d].recv()
        for (half, _), r in S.items():
            if half == h:
                r.recv()

        def group(gi, carry):
            for w in range(2):
                def gather(i, carry2):
                    k = lax.rem(m + gi * 16 + i, NM)
                    b = perm_ref[w, k]
                    cc = lax.rem(b, NC)
                    zz = lax.rem(lax.div(b, NC), NZ)
                    yy = lax.div(b, NC * NZ)
                    o = lax.rem(zz + NZ - z, NZ)
                    rows = pl.ds(pl.multiple_of(i * HALF, HALF), HALF)
                    if h == 0:
                        lhs[w, :, rows, :] = tt0[cc, yy, slot_of(o)]
                    else:
                        lhs[w, :, rows, :] = tt1[cc, slot_of(o), yy]
                    for j in range(2):
                        fs[w, j, rows, :] = jnp.broadcast_to(
                            facx[w, j, pl.ds(b, 1), :], (HALF, 128)
                        )
                    return carry2

                lax.fori_loop(0, 16, gather, 0, unroll=True)
                tot = None
                for p in range(NX):
                    r = jnp.dot(lhs[w, p], G[p, w], preferred_element_type=F32)
                    v = r[:, :128] * fs[w, 0] + r[:, 128:] * fs[w, 1]
                    v = jnp.clip(v, -1.0, 1.0).astype(BF).astype(F32)
                    tot = v if tot is None else tot + v
                abuf[h, pl.ds(gi * 16, 16), w] = tot.astype(BF).reshape(16, HALF, 128)

            def push(i, carry2):
                k = lax.rem(m + i, NM)

                @pl.when(i > 0)
                def _():
                    pltpu.make_async_remote_copy(
                        src_ref=abuf.at[h, i], dst_ref=recv_ref.at[h, m],
                        send_sem=a_ss.at[h], recv_sem=a_rs.at[h],
                        device_id=(q, k), device_id_type=MESH,
                    ).start()

                return carry2

            lax.fori_loop(gi * 16, gi * 16 + 16, push, 0)
            return carry

        lax.fori_loop(g0, g1, group, 0)
        if g0 == 0:
            cp = pltpu.make_async_copy(abuf.at[h, 0], recv_ref.at[h, m], lsem.at[6 + h])
            cp.start()
            own.append((h, cp))

    ops = {
        "xt": x_tokens, "zs": z_start, "y": y_first, "o": y_second, "b": sibling,
        "ys": y_start, "k": k_step, "bk": k_sibling,
        "ga": act_grads, "gx": x_grads, "mk": masks, "il": ig_load, "i": ig_chunk,
        "c": core_sum, "r1": rs_first, "r2": rs_second, "rz": rs_z, "w": wgrad,
    }
    for name, *args in SCHEDULE:
        ops[name](*args)

    for h, cp in own:
        cp.wait()
        done = pltpu.make_async_remote_copy(
            src_ref=abuf.at[h, pl.ds(1, NM - 1)], dst_ref=recv_ref.at[h, pl.ds(0, NM - 1)],
            send_sem=a_ss.at[h], recv_sem=a_rs.at[h], device_id=dev_sib, device_id_type=MESH,
        )
        done.wait_recv()
        done.wait_send()
    for r in sent:
        r.recv()
        r.copy.wait_send()


def expand(recv_ref, fac_ref, igt_ref, out_ref, ig_ref, obuf, osem):
    n = 4
    per = NM // n
    outs = []
    for g in range(n):
        for i in range(g * per, (g + 1) * per):
            for w in range(2):
                for h in range(2):
                    v = recv_ref[h, i, w].astype(F32)
                    for j in range(2):
                        col = (i * 2 + j) * 128
                        f = fac_ref[w, i * 2 + j : i * 2 + j + 1, :]
                        obuf[w, h * HALF : (h + 1) * HALF, col : col + 128] = v * f
        cols = pl.ds(g * per * 256, per * 256)
        cp = pltpu.make_async_copy(obuf.at[:, :, cols], out_ref.at[:, :, cols], osem.at[g])
        cp.start()
        outs.append(cp)
    ig_ref[...] = igt_ref[...].T.astype(BF)
    for cp in outs:
        cp.wait()


def body(tokens, gate_act, up_act, hidden_grad, gate_weight, up_weight, block_mask, row_perm, scale_exp):
    any_spec = pl.BlockSpec(memory_space=pl.ANY)
    vm = pl.BlockSpec(memory_space=pltpu.VMEM)
    V = pltpu.VMEM
    igt, recv, fac = pl.pallas_call(
        kernel,
        out_shape=(
            V((128, 256), F32),
            V((2, NM, 2, HALF, 128), BF),
            V((2, 128, 128), F32),
        ),
        in_specs=[any_spec] * 9,
        out_specs=(vm, any_spec, vm),
        scratch_shapes=[
            V((2, NM, 128), jnp.int32), pltpu.SMEM((2, NM), jnp.int32), V((2, NM, 128), jnp.int32),
            V((256, 128), BF), V((256, 256), BF), V((256, 256), BF), V((256, 256), BF),
            V((8192, 256), BF), V((8192, 256), BF),
            V((2, NX, HALF, 256), BF),
            V((2, NY, NZ, NX, HALF, 256), BF), V((2, NZ, NY, NX, HALF, 256), BF),
            V((NX, 2, 256, 256), BF), V((512, 256), BF),
            V((2, NM, 256), F32), V((2, 2, NM, 128), F32),
            V((2, NX, 256, 256), BF), V((2, 2, 256, 128), F32),
            V((2, NM, 2, HALF, 128), BF),
            V((2, NY, NZ, 128, 256), BF), V((NY, NZ, 128, 256), BF), V((NY, NZ, 128, 256), BF),
            V((4, 128, 256), BF), V((4, 128, 256), BF), V((NZ, 128, 256), BF), V((NZ, 128, 256), BF),
            V((64, 256), BF), V((64, 256), BF), V((2, 3, 128, 256), BF),
            pltpu.SemaphoreType.DMA((N_SEM,)), pltpu.SemaphoreType.DMA((N_SEM,)),
            pltpu.SemaphoreType.DMA((2,)), pltpu.SemaphoreType.DMA((2,)),
            pltpu.SemaphoreType.DMA((11,)),
        ],
        compiler_params=pltpu.CompilerParams(
            collective_id=0, has_side_effects=True, vmem_limit_bytes=56 << 20
        ),
        name="grads",
    )(tokens, gate_act, up_act, hidden_grad, gate_weight, up_weight, block_mask, row_perm, scale_exp)
    out, ig = pl.pallas_call(
        expand,
        out_shape=(
            jax.ShapeDtypeStruct((2, 32, 16384), F32),
            jax.ShapeDtypeStruct((256, 128), BF),
        ),
        in_specs=[vm, vm, vm],
        out_specs=(any_spec, vm),
        scratch_shapes=[
            V((2, 32, 16384), F32), pltpu.SemaphoreType.DMA((4,)),
        ],
        compiler_params=pltpu.CompilerParams(vmem_limit_bytes=32 << 20),
        name="expand",
    )(recv, fac, igt)
    return ig, out


def solution(mesh):
    act = P("dp", "mp")
    weight = P(None, "mp")
    in_specs = (act, act, act, act, weight, weight, P(), P(), P())
    out_specs = (act, P(None, ("mp", "dp"), None))
    return jax.shard_map(body, mesh=mesh, in_specs=in_specs, out_specs=out_specs, check_vma=False)
```
